512 devices in a mesh: col: 8 (over z_hi, x), row: 64 (over z_lo, y, core).
Axes of the slice: x: 4, y: 4, z: 16 (z_hi: 2, z_lo: 8; z = z_hi * 8 + z_lo), core: 2. Of those that a mesh axis runs over, the one named last changes fastest.
Arguments:
- matrix: float32 [65536, 2048], P('row', 'col'), may hold values from -130 to 130
- keep: int32 [8, 256], P('col'), may hold values from 0 to 255, as said below
Outputs:
- rotated: float32 [65536, 2048], P('row', 'col')
- col_norms: float32 [2048], P('col')
The draws below stay inside these ranges and needn't reach their ends.
Inputs may be any that keep to these rules, and one draw needn't show every extreme that they name: `keep`: each row is a permutation of 0 .. 255.
All inputs are finite; a program needn't handle non-finite values.
Results may differ from the reference program's by a relative error of at most 0.00022.
Values sent between devices are 32-bit elements; how exact they have to be, the bound alone decides.
No kernel may reach another device: no remote copies, remote signals or barrier semaphores. Data moves between devices by JAX's collectives and lax.ppermute only.
A program may use at most 64 MiB of HBM per device.

```python
import math
import jax
import jax.numpy as jnp
from jax import lax

BLOCK = 128
SWEEPS = 4
ROWS = 65536
COLUMNS = 2048
N_COL = 8


def draw_matrix(key, part):
    key = jax.random.fold_in(key, 11)
    keys = jax.random.split(key, 7)
    noise = jnp.clip(jax.random.normal(keys[0], (ROWS, COLUMNS), jnp.float32), -4.0, 4.0)
    common = 0.6
    banded = noise + 0.5 * jnp.roll(noise, 1, axis=1) - 0.35 * jnp.roll(noise, 5, axis=1)
    frac = (jnp.arange(ROWS, dtype=jnp.float32) / ROWS)[:, None]
    first = jnp.clip(jax.random.normal(keys[1], (ROWS, 1), jnp.float32), -3.0, 3.0)
    second = jnp.clip(jax.random.normal(keys[2], (ROWS, 1), jnp.float32), -3.0, 3.0)
    dir_one = jax.random.uniform(keys[3], (1, COLUMNS), jnp.float32, 0.5, 1.5)
    dir_two = jax.random.uniform(keys[4], (1, COLUMNS), jnp.float32, -1.5, 1.5)
    row_scale = (1.0 + 2.0 * frac) * jnp.exp(jax.random.uniform(keys[5], (ROWS, 1), jnp.float32, 0.0, math.log(4.0))) / 4.0
    col_scale = jnp.exp(jax.random.uniform(keys[6], (1, COLUMNS), jnp.float32, 0.0, math.log(10.0))) / 3.0
    shared = (1.0 - frac) * first * dir_one + frac * second * dir_two
    return row_scale * col_scale * (banded + common * shared)


def draw_keep(key, part):
    key = jax.random.fold_in(key, 23)
    keys = jax.random.split(key, N_COL)
    orders = jax.vmap(lambda single: jax.random.permutation(single, 2 * BLOCK))(keys)
    return orders.astype(jnp.int32)


def setup_inputs(seed: int = 0) -> dict:
    arg_keys = jax.random.split(jax.random.key(seed), 3)
    return {
        "matrix": draw_matrix(jax.random.fold_in(arg_keys[2], 71), 0),
        "keep": draw_keep(jax.random.fold_in(arg_keys[2], 71), 0),
    }


STEP_GAIN = 3.0
EPSILON = 1e-06

def product(left, right):
    return jnp.dot(left, right, precision=lax.Precision.HIGHEST, preferred_element_type=jnp.float32)

def sweeps(gram):
    width = gram.shape[0]
    scale = jnp.trace(gram) / width
    scaled = gram / scale
    ladder = (jnp.arange(width, dtype=jnp.float32) - (width - 1) / 2.0) / width
    ident = jnp.eye(width, dtype=jnp.float32)
    basis = ident
    for sweep in range(SWEEPS):
        skew = STEP_GAIN / width * (scaled * ladder[None, :] - ladder[:, None] * scaled)
        turn = ident + skew + 0.5 * product(skew, skew)
        scaled = product(product(turn.T, scaled), turn)
        basis = product(basis, turn)
    return basis

def one_round(pair):
    gram = product(pair.T, pair)
    return product(pair, sweeps(gram))

def pick_columns(block, order):
    return block[:, order]

def reference(matrix, keep):
    pairs = matrix.reshape(ROWS, N_COL, 2 * BLOCK).transpose(1, 0, 2)
    first = lax.map(one_round, pairs)
    reordered = jax.vmap(pick_columns)(first, keep.astype(jnp.int32))
    kept = reordered[:, :, :BLOCK]
    given = reordered[:, :, BLOCK:]
    arrived = jnp.roll(given, 1, axis=0)
    second = lax.map(one_round, jnp.concatenate([kept, arrived], axis=2))
    col_norms = jnp.sqrt(lax.optimization_barrier(jnp.mean(second * second, axis=1)) + EPSILON).reshape(COLUMNS)
    rotated = second.transpose(1, 0, 2).reshape(ROWS, COLUMNS)
    return (rotated, col_norms)
```

```python
import jax
import jax.numpy as jnp
from jax import lax
from jax.sharding import Mesh, PartitionSpec as P

SWEEPS = 4


STEP_GAIN = 3.0
EPSILON = 1e-06

NEAR = ("y", "core")
FAR = "z_lo"
ROW = ("z_lo", "y", "core")
COL = ("z_hi", "x")


def from_behind(shard, axis, by):
    peers = lax.axis_size(axis)
    return lax.ppermute(shard, axis, [(i, (i + by) % peers) for i in range(peers)])


def product(left, right):
    return jnp.dot(left, right, precision=lax.Precision.HIGHEST, preferred_element_type=jnp.float32)


def inner_gram(left, right):
    return lax.dot_general(
        left,
        right,
        (((0,), (0,)), ((), ())),
        precision=lax.Precision.HIGHEST,
        preferred_element_type=jnp.float32,
    )


def spread(piece, axis):
    peers = lax.axis_size(axis)
    copies = jnp.broadcast_to(piece[None], (peers,) + piece.shape)
    return lax.all_to_all(copies, axis, 0, 0, tiled=True)


def row_sum(part):
    near = lax.axis_size(NEAR)
    slices = part.reshape(near, part.shape[0] // near, part.shape[1])
    mine = jnp.sum(lax.all_to_all(slices, NEAR, 0, 0, tiled=True), axis=0)
    mine = jnp.sum(spread(mine, FAR), axis=0)
    return spread(mine, NEAR).reshape(part.shape)


def sweeps(gram):
    width = gram.shape[0]
    scale = jnp.trace(gram) / width
    scaled = gram / scale
    ladder = (jnp.arange(width, dtype=jnp.float32) - (width - 1) / 2.0) / width
    ident = jnp.eye(width, dtype=jnp.float32)
    basis = ident
    for sweep in range(SWEEPS):
        skew = STEP_GAIN / width * (scaled * ladder[None, :] - ladder[:, None] * scaled)
        turn = ident + skew + 0.5 * product(skew, skew)
        scaled = inner_gram(turn, product(scaled, turn))
        basis = product(basis, turn)
    return (basis, scaled * scale)


def shards(matrix, keep):
    width = matrix.shape[1]
    half = width // 2
    gram = row_sum(inner_gram(matrix, matrix))
    basis, moved = sweeps(gram)
    order = keep[0]
    selector = (jnp.arange(width, dtype=jnp.int32)[:, None] == order[None, :]).astype(jnp.float32)
    reordered = product(matrix, product(basis, selector))
    kept = reordered[:, :half]
    moved = inner_gram(selector, product(moved, selector))
    arrived = from_behind(reordered[:, half:], COL, 1)
    arrived_gram = from_behind(moved[half:, half:], COL, 1)
    cross = row_sum(inner_gram(kept, arrived))
    gram_two = jnp.block([[moved[:half, :half], cross], [cross.T, arrived_gram]])
    basis_two, moved_two = sweeps(gram_two)
    rotated = product(kept, basis_two[:half]) + product(arrived, basis_two[half:])
    total_rows = rotated.shape[0] * lax.axis_size(ROW)
    squares = jnp.maximum(jnp.diagonal(moved_two), 0.0)
    col_norms = jnp.sqrt(squares / total_rows + EPSILON)
    return (rotated, col_norms)


def solution(mesh):
    fine = Mesh(mesh.devices.reshape(2, 4, 8, 4, 2), ("z_hi", "x", "z_lo", "y", "core"))
    return jax.shard_map(
        shards,
        mesh=fine,
        in_specs=(P(ROW, COL), P(COL, None)),
        out_specs=(P(ROW, COL), P(COL)),
        check_vma=False,
    )
```

```python
import functools

import jax
import jax.numpy as jnp
from jax import lax
from jax.sharding import Mesh, PartitionSpec as P

SWEEPS = 4


STEP_GAIN = 3.0
EPSILON = 1e-06

NEAR = ("y", "core")
FAR = "z_lo"
ROW = ("z_lo", "y", "core")
COL = ("z_hi", "x")


DIRECT, RING, TWO, ONE = 304, 240, 240, 240


def send(shard, pairs):
    return lax.ppermute(shard, COL, pairs)


def inside(source, target):
    return [(source, target), (4 + source, 4 + target)]


def across(source, target):
    return [(source, 4 + target), (4 + source, target)]


def product(left, right):
    return jnp.dot(left, right, precision=lax.Precision.HIGHEST, preferred_element_type=jnp.float32)


def inner_gram(left, right):
    return lax.dot_general(
        left,
        right,
        (((0,), (0,)), ((), ())),
        precision=lax.Precision.HIGHEST,
        preferred_element_type=jnp.float32,
    )


def spread(piece, axis):
    peers = lax.axis_size(axis)
    copies = jnp.broadcast_to(piece[None], (peers,) + piece.shape)
    return lax.all_to_all(copies, axis, 0, 0, tiled=True)


def near_sum(part):
    near = lax.axis_size(NEAR)
    slices = part.reshape(near, part.shape[0] // near, part.shape[1])
    return jnp.sum(lax.all_to_all(slices, NEAR, 0, 0, tiled=True), axis=0)


def far_sum(piece):
    return jnp.sum(spread(piece, FAR), axis=0)


def sweeps(gram):
    width = gram.shape[0]
    scale = jnp.trace(gram) / width
    scaled = gram / scale
    ladder = (jnp.arange(width, dtype=jnp.float32) - (width - 1) / 2.0) / width
    ident = jnp.eye(width, dtype=jnp.float32)
    basis = ident
    for sweep in range(SWEEPS):
        skew = STEP_GAIN / width * (scaled * ladder[None, :] - ladder[:, None] * scaled)
        turn = ident + skew + 0.5 * product(skew, skew)
        scaled = inner_gram(turn, product(scaled, turn))
        basis = product(basis, turn)
    return (basis, scaled * scale)


def shards(matrix, keep):
    rows, width = matrix.shape
    half = width // 2
    place = lax.axis_index("x")
    order = keep[0]
    selector = (jnp.arange(width, dtype=jnp.int32)[:, None] == order[None, :]).astype(jnp.float32)

    direct, ring, two, one = jnp.split(matrix, [DIRECT, DIRECT + RING, DIRECT + RING + TWO])
    turned = send(ring, sum([inside(i, (i + 1) % 4) for i in range(4)], []))
    at_two = send(two, inside(3, 2))
    at_one = send(one, inside(3, 1))
    direct = send(direct, [(i, (i + 1) % 8) for i in range(8)])
    slices = near_sum(inner_gram(matrix, matrix))
    turned, at_two, at_one, slices = lax.optimization_barrier((turned, at_two, at_one, slices))
    crossed_two = send(at_two, across(2, 0))
    crossed_one = send(at_one, across(1, 0))
    crossed_ring = send(turned, across(0, 0))
    shifted = send(matrix[DIRECT + RING :], sum([inside(i, i + 1) for i in range(3)], []))

    def turn_first(slices):
        gram = spread(far_sum(slices), NEAR).reshape(width, width)
        basis, moved = sweeps(gram)
        reordered = product(basis, selector)
        moved = inner_gram(selector, product(moved, selector))
        given = jnp.concatenate([reordered[:, half:], moved[half:, half:]], axis=0)
        share = given.shape[0] // lax.axis_size(NEAR)
        mine = lax.dynamic_slice_in_dim(given, lax.axis_index(NEAR) * share, share, 0)
        return (reordered[:, :half], moved[:half, :half], mine)

    blank = functools.partial(jnp.zeros, dtype=jnp.float32)
    kept_basis, kept_gram, mine = lax.cond(
        order[0] >= 0,
        turn_first,
        lambda slices: (blank((width, half)), blank((half, half)), blank((48, half))),
        slices,
    )
    mine = send(mine, [(i, (i + 1) % 8) for i in range(8)])

    direct, turned, crossed_two, crossed_one, crossed_ring, shifted, kept_basis = lax.optimization_barrier(
        (direct, turned, crossed_two, crossed_one, crossed_ring, shifted, kept_basis)
    )
    first = place == 0
    behind = jnp.concatenate(
        [
            direct,
            jnp.where(first, crossed_ring, turned),
            jnp.where(first, crossed_two, shifted[:TWO]),
            jnp.where(first, crossed_one, shifted[TWO:]),
        ],
        axis=0,
    )
    cross = near_sum(inner_gram(behind, matrix))
    cross = far_sum(product(cross, kept_basis))
    both = spread(jnp.concatenate([cross, mine], axis=0), NEAR)
    cut = cross.shape[0]
    cross = both[:, :cut].reshape(width, half)
    given = both[:, cut:].reshape(width + half, half)
    given_basis, given_gram = given[:width], given[width:]
    cross = inner_gram(given_basis, cross)
    gram_two = jnp.block([[kept_gram, cross.T], [cross, given_gram]])
    basis_two, gram_three = sweeps(gram_two)
    rotated = product(matrix, product(kept_basis, basis_two[:half])) + product(
        behind, product(given_basis, basis_two[half:])
    )
    ident = jnp.eye(width, dtype=jnp.float32)
    squares = jnp.maximum(jnp.sum(gram_three * ident, axis=0), 0.0)
    col_norms = jnp.sqrt(squares / (rows * lax.axis_size(ROW)) + EPSILON)
    return (rotated, col_norms)


def solution(mesh):
    fine = Mesh(mesh.devices.reshape(2, 4, 8, 4, 2), ("z_hi", "x", "z_lo", "y", "core"))
    return jax.shard_map(
        shards,
        mesh=fine,
        in_specs=(P(ROW, COL), P(COL, None)),
        out_specs=(P(ROW, COL), P(COL)),
        check_vma=False,
    )
```

```python
import functools

import jax
import jax.numpy as jnp
from jax import lax
from jax.experimental import pallas as pl
from jax.experimental.pallas import tpu as pltpu
from jax.sharding import Mesh, PartitionSpec as P

SWEEPS = 4


STEP_GAIN = 3.0
EPSILON = 1e-06

NEAR = ("y", "core")
FAR = "z_lo"
ROW = ("z_lo", "y", "core")
COL = ("z_hi", "x")


DIRECT, RING, TWO, ONE = 304, 240, 240, 240


def send(shard, pairs):
    return lax.ppermute(shard, COL, pairs)


def inside(source, target):
    return [(source, target), (4 + source, 4 + target)]


def across(source, target):
    return [(source, 4 + target), (4 + source, target)]


def product(left, right):
    return jnp.dot(left, right, precision=lax.Precision.HIGH, preferred_element_type=jnp.float32)


def inner_gram(left, right):
    return lax.dot_general(
        left,
        right,
        (((0,), (0,)), ((), ())),
        precision=lax.Precision.HIGH,
        preferred_element_type=jnp.float32,
    )


def spread(piece, axis):
    peers = lax.axis_size(axis)
    copies = jnp.broadcast_to(piece[None], (peers,) + piece.shape)
    return lax.all_to_all(copies, axis, 0, 0, tiled=True)


def near_sum(part):
    near = lax.axis_size(NEAR)
    slices = part.reshape(near, part.shape[0] // near, part.shape[1])
    return jnp.sum(lax.all_to_all(slices, NEAR, 0, 0, tiled=True), axis=0)


def far_sum(piece):
    return jnp.sum(spread(piece, FAR), axis=0)


ALONG = (((1,), (0,)), ((), ()))
DOWN = (((0,), (0,)), ((), ()))


def halves(value):
    high = value.astype(jnp.bfloat16)
    return high, (value - high.astype(jnp.float32)).astype(jnp.bfloat16)


def times(left, right, dims=ALONG):
    def dot(one, other):
        return lax.dot_general(one, other, dims, preferred_element_type=jnp.float32)

    return dot(left[0], right[0]) + (dot(left[0], right[1]) + dot(left[1], right[0]))


def picks(left, chosen, dims=ALONG):
    def dot(one):
        return lax.dot_general(one, chosen, dims, preferred_element_type=jnp.float32)

    return dot(left[0]) + dot(left[1])


def diagonal(value):
    width = value.shape[0]
    down = lax.broadcasted_iota(jnp.int32, (width, width), 0)
    along = lax.broadcasted_iota(jnp.int32, (width, width), 1)
    return jnp.where(down == along, value, 0.0)


def swept(gram, last_gram):
    width = gram.shape[0]
    scale = jnp.sum(jnp.sum(diagonal(gram), axis=0, keepdims=True), axis=1, keepdims=True) / width
    scaled = gram / scale
    down = lax.broadcasted_iota(jnp.int32, (width, width), 0)
    along = lax.broadcasted_iota(jnp.int32, (width, width), 1)
    steps = (along - down).astype(jnp.float32) * (STEP_GAIN / width / width)
    ident = jnp.where(down == along, 1.0, 0.0)
    basis = ident
    for sweep in range(SWEEPS):
        skew = scaled * steps
        pair = halves(skew)
        square = 0.5 * times(pair, pair)
        move = skew + square
        moves = halves(move)
        half_way = scaled + times(halves(scaled), moves)
        basis = ident + move if sweep == 0 else basis + times(halves(basis), moves)
        if sweep < SWEEPS - 1 or last_gram:
            scaled = half_way + times(halves(square - skew), halves(half_way))
    if last_gram:
        return basis, scaled * scale
    return basis, jnp.sum((ident + move) * half_way, axis=0, keepdims=True) * scale


def whole_gram(upper, between, lower):
    return jnp.concatenate(
        [
            jnp.concatenate([upper, between], axis=1),
            jnp.concatenate([between.T, lower], axis=1),
        ],
        axis=0,
    )


def picked(blocks, order, first):
    half = blocks.shape[1]
    gram = whole_gram(blocks[:half], blocks[half : 2 * half], blocks[2 * half :])
    basis, moved = swept(gram, True)
    down = lax.broadcasted_iota(jnp.int32, (2 * half, half), 0)
    chosen = jnp.where(down == order[:, first : first + half], 1.0, 0.0).astype(jnp.bfloat16)
    columns = halves(picks(halves(moved), chosen))
    return picks(halves(basis), chosen), picks(columns, chosen, DOWN)


def first_kernel(blocks_ref, order_ref, kept_ref, gram_ref):
    half = blocks_ref.shape[2]
    kept_ref[...], gram_ref[...] = picked(blocks_ref[...].reshape(3 * half, half), order_ref[...], 0)


def sweep_first(blocks, order):
    half = blocks.shape[2]
    return pl.pallas_call(
        first_kernel,
        out_shape=(
            jax.ShapeDtypeStruct((2 * half, half), jnp.float32),
            jax.ShapeDtypeStruct((half, half), jnp.float32),
        ),
        compiler_params=pltpu.CompilerParams(vmem_limit_bytes=40 * 2**20),
        name="sweep_first",
    )(blocks, order)


def last_kernel(rows, sums_ref, order_ref, kept_ref, gram_ref, own_ref, behind_ref,
                out_ref, norm_ref, own_high, own_low, behind_high, behind_low):
    half = kept_ref.shape[1]
    share = 2 * half // sums_ref.shape[0]

    @pl.when(pl.program_id(0) == 0)
    def _():
        given, given_gram = picked(sums_ref[:, share:, :].reshape(3 * half, half), order_ref[...], half)
        given = halves(given)
        cross = halves(sums_ref[:, :share, :].reshape(2 * half, half))
        between = times(cross, given, DOWN)
        basis, squares = swept(whole_gram(gram_ref[...], between, given_gram), False)
        norm_ref[...] = jnp.sqrt(jnp.maximum(squares, 0.0) / rows + EPSILON)
        own_high[...], own_low[...] = halves(times(halves(kept_ref[...]), halves(basis[:half])))
        behind_high[...], behind_low[...] = halves(times(given, halves(basis[half:])))

    out_ref[...] = times(halves(own_ref[...]), (own_high[...], own_low[...])) + times(
        halves(behind_ref[...]), (behind_high[...], behind_low[...])
    )


def sweep_last(rows, sums, order, kept, gram, own, behind):
    width = own.shape[1]
    tile = 256
    full = lambda value: pl.BlockSpec(value.shape, lambda step: (0,) * value.ndim)
    tiles = pl.BlockSpec((tile, width), lambda step: (step, 0))
    small = (sums, order, kept, gram)
    return pl.pallas_call(
        functools.partial(last_kernel, rows),
        grid=(own.shape[0] // tile,),
        in_specs=[full(value) for value in small] + [tiles, tiles],
        out_specs=(tiles, pl.BlockSpec((1, width), lambda step: (0, 0))),
        out_shape=(jax.ShapeDtypeStruct(own.shape, jnp.float32), jax.ShapeDtypeStruct((1, width), jnp.float32)),
        scratch_shapes=[pltpu.VMEM((width, width), jnp.bfloat16)] * 4,
        compiler_params=pltpu.CompilerParams(vmem_limit_bytes=40 * 2**20),
        name="sweep_last",
    )(*small, own, behind)


def first_blocks(matrix):
    half = matrix.shape[1] // 2
    top = inner_gram(matrix[:, :half], matrix)
    return jnp.concatenate(
        [top[:, :half], top[:, half:], inner_gram(matrix[:, half:], matrix[:, half:])], axis=0
    )


def shards(matrix, keep):
    rows, width = matrix.shape
    half = width // 2
    place = lax.axis_index("x")
    part, whole = lax.optimization_barrier((first_blocks(matrix), matrix))
    direct, _, two, one = jnp.split(whole, [DIRECT, DIRECT + RING, DIRECT + RING + TWO])
    turned = send(whole[DIRECT:], sum([inside(i, (i + 1) % 4) for i in range(4)], []))
    at_two = send(two, inside(3, 2))
    at_one = send(one, inside(3, 1))
    slices = near_sum(part)
    turned, at_two, at_one, slices = lax.optimization_barrier((turned, at_two, at_one, slices))
    crossed_two = send(at_two, across(2, 0))
    crossed_one = send(at_one, across(1, 0))
    crossed_ring = send(turned[:RING], across(0, 0))
    direct = send(direct, [(i, (i + 1) % 8) for i in range(8)])
    slices = far_sum(slices)
    share = slices.shape[0]
    order = jnp.broadcast_to(keep.astype(jnp.float32).reshape(2, half)[None], (4, 2, half)).reshape(8, half)
    arrived = send(jnp.concatenate([slices, order], axis=0), [(i, (i + 1) % 8) for i in range(8)])

    def turn_first(slices, keep):
        return sweep_first(spread(slices, NEAR), keep)

    kept_basis, kept_gram = lax.cond(
        keep[0, 0] >= 0,
        turn_first,
        lambda *_: (jnp.zeros((width, half), jnp.float32), jnp.zeros((half, half), jnp.float32)),
        slices,
        keep,
    )

    direct, crossed_ring, crossed_two, crossed_one, arrived, kept_basis = lax.optimization_barrier(
        (direct, crossed_ring, crossed_two, crossed_one, arrived, kept_basis)
    )
    crossed = jnp.concatenate([crossed_ring, crossed_two, crossed_one], axis=0)
    behind = jnp.concatenate([direct, jnp.where(place == 0, crossed, turned)], axis=0)
    cross = far_sum(product(near_sum(inner_gram(behind, matrix)), kept_basis))
    sums = spread(jnp.concatenate([cross, arrived[:share]], axis=0), NEAR)
    behind_keep = arrived[share : share + 2].reshape(1, width).astype(jnp.int32)
    total_rows = rows * lax.axis_size(ROW)
    rotated, norms = sweep_last(total_rows, sums, behind_keep, kept_basis, kept_gram, matrix, behind)
    return (rotated, norms.reshape(width))


def solution(mesh):
    fine = Mesh(mesh.devices.reshape(2, 4, 8, 4, 2), ("z_hi", "x", "z_lo", "y", "core"))
    return jax.shard_map(
        shards,
        mesh=fine,
        in_specs=(P(ROW, COL), P(COL, None)),
        out_specs=(P(ROW, COL), P(COL)),
        check_vma=False,
    )
```

```python
import functools

import jax
import jax.numpy as jnp
from jax import lax
from jax.experimental import pallas as pl
from jax.experimental.pallas import tpu as pltpu
from jax.sharding import Mesh, PartitionSpec as P

SWEEPS = 4


STEP_GAIN = 3.0
EPSILON = 1e-06

NEAR = ("y", "core")
FAR = "z_lo"
ROW = ("z_lo", "y", "core")
COL = ("z_hi", "x")


DIRECT, RING, TWO, ONE = 216, 256, 280, 272


def send(shard, pairs):
    return lax.ppermute(shard, COL, pairs)


def inside(source, target):
    return [(source, target), (4 + source, 4 + target)]


def across(source, target):
    return [(source, 4 + target), (4 + source, target)]


def product(left, right):
    return jnp.dot(left, right, precision=lax.Precision.HIGH, preferred_element_type=jnp.float32)


def inner_gram(left, right):
    return lax.dot_general(
        left,
        right,
        (((0,), (0,)), ((), ())),
        precision=lax.Precision.HIGH,
        preferred_element_type=jnp.float32,
    )


def spread(piece, axis):
    peers = lax.axis_size(axis)
    copies = jnp.broadcast_to(piece[None], (peers,) + piece.shape)
    return lax.all_to_all(copies, axis, 0, 0, tiled=True)


def near_sum(part):
    near = lax.axis_size(NEAR)
    slices = part.reshape(near, part.shape[0] // near, part.shape[1])
    return jnp.sum(lax.all_to_all(slices, NEAR, 0, 0, tiled=True), axis=0)


def far_sum(piece):
    return jnp.sum(spread(piece, FAR), axis=0)


ALONG = (((1,), (0,)), ((), ()))
DOWN = (((0,), (0,)), ((), ()))


def halves(value):
    high = value.astype(jnp.bfloat16)
    return high, (value - high.astype(jnp.float32)).astype(jnp.bfloat16)


def times(left, right, dims=ALONG):
    def dot(one, other):
        return lax.dot_general(one, other, dims, preferred_element_type=jnp.float32)

    return dot(left[0], right[0]) + (dot(left[0], right[1]) + dot(left[1], right[0]))


def picks(left, chosen, dims=ALONG):
    def dot(one):
        return lax.dot_general(one, chosen, dims, preferred_element_type=jnp.float32)

    return dot(left[0]) + dot(left[1])


def diagonal(value):
    width = value.shape[0]
    down = lax.broadcasted_iota(jnp.int32, (width, width), 0)
    along = lax.broadcasted_iota(jnp.int32, (width, width), 1)
    return jnp.where(down == along, value, 0.0)


def swept(gram, last_gram):
    width = gram.shape[0]
    scale = jnp.sum(jnp.sum(diagonal(gram), axis=0, keepdims=True), axis=1, keepdims=True) / width
    scaled = gram / scale
    down = lax.broadcasted_iota(jnp.int32, (width, width), 0)
    along = lax.broadcasted_iota(jnp.int32, (width, width), 1)
    steps = (along - down).astype(jnp.float32) * (STEP_GAIN / width / width)
    ident = jnp.where(down == along, 1.0, 0.0)
    basis = ident
    for sweep in range(SWEEPS):
        skew = scaled * steps
        pair = halves(skew)
        square = 0.5 * times(pair, pair)
        move = skew + square
        moves = halves(move)
        half_way = scaled + times(halves(scaled), moves)
        basis = ident + move if sweep == 0 else basis + times(halves(basis), moves)
        if sweep < SWEEPS - 1 or last_gram:
            scaled = half_way + times(halves(square - skew), halves(half_way))
    if last_gram:
        return basis, scaled * scale
    return basis, jnp.sum((ident + move) * half_way, axis=0, keepdims=True) * scale


def whole_gram(upper, between, lower):
    return jnp.concatenate(
        [
            jnp.concatenate([upper, between], axis=1),
            jnp.concatenate([between.T, lower], axis=1),
        ],
        axis=0,
    )


def picked(blocks, order, first):
    half = blocks.shape[1]
    gram = whole_gram(blocks[:half], blocks[half : 2 * half], blocks[2 * half :])
    basis, moved = swept(gram, True)
    down = lax.broadcasted_iota(jnp.int32, (2 * half, half), 0)
    chosen = jnp.where(down == order[:, first : first + half], 1.0, 0.0).astype(jnp.bfloat16)
    columns = halves(picks(halves(moved), chosen))
    return picks(halves(basis), chosen), picks(columns, chosen, DOWN)


def turn_kernel(first, blocks_ref, order_ref, basis_ref, gram_ref):
    half = blocks_ref.shape[2]
    basis_ref[...], gram_ref[...] = picked(blocks_ref[...].reshape(3 * half, half), order_ref[...], first)


def turn_pair(blocks, order, first):
    half = blocks.shape[2]
    return pl.pallas_call(
        functools.partial(turn_kernel, first),
        out_shape=(
            jax.ShapeDtypeStruct((2 * half, half), jnp.float32),
            jax.ShapeDtypeStruct((half, half), jnp.float32),
        ),
        compiler_params=pltpu.CompilerParams(vmem_limit_bytes=40 * 2**20),
        cost_estimate=pl.CostEstimate(flops=5 * 10**9, bytes_accessed=4 * 10**5, transcendentals=0),
        name="turn_pair",
    )(blocks, order)


def last_kernel(rows, cross_ref, kept_ref, gram_ref, given_ref, given_gram_ref, own_ref, behind_ref,
                out_ref, norm_ref, own_high, own_low, behind_high, behind_low):
    half = kept_ref.shape[1]

    @pl.when(pl.program_id(0) == 0)
    def _():
        given = halves(given_ref[...])
        between = times(halves(cross_ref[...].reshape(2 * half, half)), given, DOWN)
        basis, squares = swept(whole_gram(gram_ref[...], between, given_gram_ref[...]), False)
        norm_ref[...] = jnp.sqrt(jnp.maximum(squares, 0.0) / rows + EPSILON)
        own_high[...], own_low[...] = halves(times(halves(kept_ref[...]), halves(basis[:half])))
        behind_high[...], behind_low[...] = halves(times(given, halves(basis[half:])))

    out_ref[...] = times(halves(own_ref[...]), (own_high[...], own_low[...])) + times(
        halves(behind_ref[...]), (behind_high[...], behind_low[...])
    )


def sweep_last(rows, cross, kept, gram, given, given_gram, own, behind):
    width = own.shape[1]
    tile = 256
    full = lambda value: pl.BlockSpec(value.shape, lambda step: (0,) * value.ndim)
    tiles = pl.BlockSpec((tile, width), lambda step: (step, 0))
    small = (cross, kept, gram, given, given_gram)
    return pl.pallas_call(
        functools.partial(last_kernel, rows),
        grid=(own.shape[0] // tile,),
        in_specs=[full(value) for value in small] + [tiles, tiles],
        out_specs=(tiles, pl.BlockSpec((1, width), lambda step: (0, 0))),
        out_shape=(jax.ShapeDtypeStruct(own.shape, jnp.float32), jax.ShapeDtypeStruct((1, width), jnp.float32)),
        scratch_shapes=[pltpu.VMEM((width, width), jnp.bfloat16)] * 4,
        compiler_params=pltpu.CompilerParams(vmem_limit_bytes=40 * 2**20),
        name="sweep_last",
    )(*small, own, behind)


def first_blocks(matrix):
    half = matrix.shape[1] // 2
    gram = inner_gram(matrix, matrix)
    return jnp.concatenate([gram[:half, :half], gram[:half, half:], gram[half:, half:]], axis=0)


def shards(matrix, keep):
    rows, width = matrix.shape
    half = width // 2
    place = lax.axis_index("x")
    part, whole = first_blocks(matrix), matrix
    direct, _, two, one = jnp.split(whole, [DIRECT, DIRECT + RING, DIRECT + RING + TWO])
    turned = send(whole[DIRECT:], sum([inside(i, (i + 1) % 4) for i in range(4)], []))
    at_two = send(two, inside(3, 2))
    at_one = send(one, inside(3, 1))
    slices = near_sum(part)
    at_two, at_one, slices = lax.optimization_barrier((at_two, at_one, slices))
    crossed_ring = send(turned[:RING], across(0, 0))
    crossed_two = send(at_two, across(2, 0))
    crossed_one = send(at_one, across(1, 0))
    direct = send(direct, [(i, (i + 1) % 8) for i in range(8)])
    slices = far_sum(slices)
    share = slices.shape[0]
    order = jnp.broadcast_to(keep.astype(jnp.float32).reshape(2, half)[None], (4, 2, half)).reshape(8, half)
    arrived = send(jnp.concatenate([slices, order], axis=0), [(i, (i + 1) % 8) for i in range(8)])

    def turn_first(slices, keep):
        return turn_pair(spread(slices, NEAR), keep, 0)

    kept_basis, kept_gram = lax.cond(
        keep[0, 0] >= 0,
        turn_first,
        lambda *_: (jnp.zeros((width, half), jnp.float32), jnp.zeros((half, half), jnp.float32)),
        slices,
        keep,
    )

    direct, crossed_ring, crossed_two, crossed_one, arrived, kept_basis = lax.optimization_barrier(
        (direct, crossed_ring, crossed_two, crossed_one, arrived, kept_basis)
    )
    crossed = jnp.concatenate([crossed_ring, crossed_two, crossed_one], axis=0)
    behind = jnp.concatenate([direct, jnp.where(place == 0, crossed, turned)], axis=0)
    near = lax.axis_size(NEAR)
    cross = inner_gram(behind, matrix)
    cut = width // near
    parts = [cross[:, :half].reshape(near, cut, half), cross[:, half:].reshape(near, cut, half)]
    parts.append(jnp.broadcast_to(arrived[None, :share], (near, share, half)))
    parts = lax.all_to_all(jnp.concatenate(parts, axis=1), NEAR, 0, 0, tiled=True)
    cross = jnp.sum(parts[:, : 2 * cut], axis=0)
    cross = product(cross[:cut], kept_basis[:half]) + product(cross[cut:], kept_basis[half:])
    behind_keep = arrived[share : share + 2].reshape(1, width).astype(jnp.int32)
    given_basis, given_gram = turn_pair(parts[:, 2 * cut :], behind_keep, half)
    rotated, norms = sweep_last(
        rows * lax.axis_size(ROW),
        spread(far_sum(cross), NEAR),
        kept_basis,
        kept_gram,
        given_basis,
        given_gram,
        matrix,
        behind,
    )
    return (rotated, norms.reshape(width))


def solution(mesh):
    fine = Mesh(mesh.devices.reshape(2, 4, 8, 4, 2), ("z_hi", "x", "z_lo", "y", "core"))
    return jax.shard_map(
        shards,
        mesh=fine,
        in_specs=(P(ROW, COL), P(COL, None)),
        out_specs=(P(ROW, COL), P(COL)),
        check_vma=False,
    )
```

```python
import functools

import jax
import jax.numpy as jnp
from jax import lax
from jax.experimental import pallas as pl
from jax.experimental.pallas import tpu as pltpu
from jax.sharding import Mesh, PartitionSpec as P

SWEEPS = 4


STEP_GAIN = 3.0
EPSILON = 1e-06

NEAR = ("y", "core")
FAR = "z_lo"
ROW = ("z_lo", "y", "core")
COL = ("z_hi", "x")


DIRECT, RING, TWO, ONE = 272, 224, 264, 264


def send(shard, pairs):
    return lax.ppermute(shard, COL, pairs)


def inside(source, target):
    return [(source, target), (4 + source, 4 + target)]


def across(source, target):
    return [(source, 4 + target), (4 + source, target)]


def product(left, right):
    return jnp.dot(left, right, precision=lax.Precision.HIGH, preferred_element_type=jnp.float32)


def inner_gram(left, right):
    return lax.dot_general(
        left,
        right,
        (((0,), (0,)), ((), ())),
        precision=lax.Precision.HIGH,
        preferred_element_type=jnp.float32,
    )


def spread(piece, axis):
    peers = lax.axis_size(axis)
    copies = jnp.broadcast_to(piece[None], (peers,) + piece.shape)
    return lax.all_to_all(copies, axis, 0, 0, tiled=True)


def near_sum(part):
    near = lax.axis_size(NEAR)
    slices = part.reshape(near, part.shape[0] // near, part.shape[1])
    return jnp.sum(lax.all_to_all(slices, NEAR, 0, 0, tiled=True), axis=0)


def far_sum(piece):
    return jnp.sum(spread(piece, FAR), axis=0)


ALONG = (((1,), (0,)), ((), ()))
DOWN = (((0,), (0,)), ((), ()))


def halves(value):
    high = value.astype(jnp.bfloat16)
    return high, (value - high.astype(jnp.float32)).astype(jnp.bfloat16)


def times(left, right, dims=ALONG):
    def dot(one, other):
        return lax.dot_general(one, other, dims, preferred_element_type=jnp.float32)

    return dot(left[0], right[0]) + (dot(left[0], right[1]) + dot(left[1], right[0]))


def picks(left, chosen, dims=ALONG):
    def dot(one):
        return lax.dot_general(one, chosen, dims, preferred_element_type=jnp.float32)

    return dot(left[0]) + dot(left[1])


def diagonal(value):
    width = value.shape[0]
    down = lax.broadcasted_iota(jnp.int32, (width, width), 0)
    along = lax.broadcasted_iota(jnp.int32, (width, width), 1)
    return jnp.where(down == along, value, 0.0)


def swept(gram, last_gram):
    width = gram.shape[0]
    scale = jnp.sum(jnp.sum(diagonal(gram), axis=0, keepdims=True), axis=1, keepdims=True) / width
    scaled = gram / scale
    down = lax.broadcasted_iota(jnp.int32, (width, width), 0)
    along = lax.broadcasted_iota(jnp.int32, (width, width), 1)
    steps = (along - down).astype(jnp.float32) * (STEP_GAIN / width / width)
    ident = jnp.where(down == along, 1.0, 0.0)
    basis = ident
    for sweep in range(SWEEPS):
        skew = scaled * steps
        pair = halves(skew)
        square = 0.5 * times(pair, pair)
        move = skew + square
        moves = halves(move)
        half_way = scaled + times(halves(scaled), moves)
        basis = ident + move if sweep == 0 else basis + times(halves(basis), moves)
        if sweep < SWEEPS - 1 or last_gram:
            scaled = half_way + times(halves(square - skew), halves(half_way))
    if last_gram:
        return basis, scaled * scale
    return basis, jnp.sum((ident + move) * half_way, axis=0, keepdims=True) * scale


def whole_gram(upper, between, lower):
    return jnp.concatenate(
        [
            jnp.concatenate([upper, between], axis=1),
            jnp.concatenate([between.T, lower], axis=1),
        ],
        axis=0,
    )


def picked(blocks, order, first):
    half = blocks.shape[1]
    gram = whole_gram(blocks[:half], blocks[half : 2 * half], blocks[2 * half :])
    basis, moved = swept(gram, True)
    down = lax.broadcasted_iota(jnp.int32, (2 * half, half), 0)
    chosen = jnp.where(down == order[:, first : first + half], 1.0, 0.0).astype(jnp.bfloat16)
    columns = halves(picks(halves(moved), chosen))
    return picks(halves(basis), chosen), picks(columns, chosen, DOWN)


def turn_kernel(first, blocks_ref, order_ref, basis_ref, gram_ref):
    half = blocks_ref.shape[2]
    basis_ref[...], gram_ref[...] = picked(blocks_ref[...].reshape(3 * half, half), order_ref[...], first)


def turn_pair(blocks, order, first):
    half = blocks.shape[2]
    return pl.pallas_call(
        functools.partial(turn_kernel, first),
        out_shape=(
            jax.ShapeDtypeStruct((2 * half, half), jnp.float32),
            jax.ShapeDtypeStruct((half, half), jnp.float32),
        ),
        compiler_params=pltpu.CompilerParams(vmem_limit_bytes=40 * 2**20),
        cost_estimate=pl.CostEstimate(flops=5 * 10**9, bytes_accessed=4 * 10**5, transcendentals=0),
        name="turn_pair",
    )(blocks, order)


def last_kernel(rows, cross_ref, kept_ref, gram_ref, given_ref, given_gram_ref, own_ref, behind_ref,
                out_ref, norm_ref, own_high, own_low, behind_high, behind_low):
    half = kept_ref.shape[1]

    @pl.when(pl.program_id(0) == 0)
    def _():
        given = halves(given_ref[...])
        between = times(halves(cross_ref[...].reshape(2 * half, half)), given, DOWN)
        basis, squares = swept(whole_gram(gram_ref[...], between, given_gram_ref[...]), False)
        norm_ref[...] = jnp.sqrt(jnp.maximum(squares, 0.0) / rows + EPSILON)
        own_high[...], own_low[...] = halves(times(halves(kept_ref[...]), halves(basis[:half])))
        behind_high[...], behind_low[...] = halves(times(given, halves(basis[half:])))

    out_ref[...] = times(halves(own_ref[...]), (own_high[...], own_low[...])) + times(
        halves(behind_ref[...]), (behind_high[...], behind_low[...])
    )


def sweep_last(rows, cross, kept, gram, given, given_gram, own, behind):
    width = own.shape[1]
    tile = 256
    full = lambda value: pl.BlockSpec(value.shape, lambda step: (0,) * value.ndim)
    tiles = pl.BlockSpec((tile, width), lambda step: (step, 0))
    small = (cross, kept, gram, given, given_gram)
    return pl.pallas_call(
        functools.partial(last_kernel, rows),
        grid=(own.shape[0] // tile,),
        in_specs=[full(value) for value in small] + [tiles, tiles],
        out_specs=(tiles, pl.BlockSpec((1, width), lambda step: (0, 0))),
        out_shape=(jax.ShapeDtypeStruct(own.shape, jnp.float32), jax.ShapeDtypeStruct((1, width), jnp.float32)),
        scratch_shapes=[pltpu.VMEM((width, width), jnp.bfloat16)] * 4,
        compiler_params=pltpu.CompilerParams(vmem_limit_bytes=40 * 2**20),
        name="sweep_last",
    )(*small, own, behind)


def first_blocks(matrix):
    half = matrix.shape[1] // 2
    gram = inner_gram(matrix, matrix)
    return jnp.concatenate([gram[:half, :half], gram[:half, half:], gram[half:, half:]], axis=0)


def shards(matrix, keep):
    rows, width = matrix.shape
    half = width // 2
    place = lax.axis_index("x")
    direct, _, two, one = jnp.split(matrix, [DIRECT, DIRECT + RING, DIRECT + RING + TWO])
    turned = send(matrix[DIRECT:], sum([inside(i, (i + 1) % 4) for i in range(4)], []))
    part, two, one = lax.optimization_barrier((first_blocks(matrix), two, one))
    at_two = send(two, inside(3, 2))
    at_one = send(one, inside(3, 1))
    slices = near_sum(part)
    at_two, at_one, slices = lax.optimization_barrier((at_two, at_one, slices))
    crossed_ring = send(turned[:RING], across(0, 0))
    crossed_two = send(at_two, across(2, 0))
    crossed_one = send(at_one, across(1, 0))
    direct = send(direct, [(i, (i + 1) % 8) for i in range(8)])
    slices = far_sum(slices)
    share = slices.shape[0]
    order = jnp.broadcast_to(keep.astype(jnp.float32).reshape(2, half)[None], (4, 2, half)).reshape(8, half)
    arrived = send(jnp.concatenate([slices, order], axis=0), [(i, (i + 1) % 8) for i in range(8)])

    def turn_first(slices, keep):
        return turn_pair(spread(slices, NEAR), keep, 0)

    kept_basis, kept_gram = lax.cond(
        keep[0, 0] >= 0,
        turn_first,
        lambda *_: (jnp.zeros((width, half), jnp.float32), jnp.zeros((half, half), jnp.float32)),
        slices,
        keep,
    )

    direct, crossed_ring, crossed_two, crossed_one, arrived, kept_basis = lax.optimization_barrier(
        (direct, crossed_ring, crossed_two, crossed_one, arrived, kept_basis)
    )
    crossed = jnp.concatenate([crossed_ring, crossed_two, crossed_one], axis=0)
    behind = jnp.concatenate([direct, jnp.where(place == 0, crossed, turned)], axis=0)
    near = lax.axis_size(NEAR)
    cut = width // near
    cross = inner_gram(behind, product(matrix, kept_basis)).reshape(near, cut, half)
    parts = [cross, jnp.broadcast_to(arrived[None, :share], (near, share, half))]
    parts = lax.all_to_all(jnp.concatenate(parts, axis=1), NEAR, 0, 0, tiled=True)
    cross = far_sum(jnp.sum(parts[:, :cut], axis=0))
    behind_keep = arrived[share : share + 2].reshape(1, width).astype(jnp.int32)
    given_basis, given_gram = turn_pair(parts[:, cut:], behind_keep, half)
    cross, given_basis, given_gram = lax.optimization_barrier((cross, given_basis, given_gram))
    rotated, norms = sweep_last(
        rows * lax.axis_size(ROW),
        spread(cross, NEAR),
        kept_basis,
        kept_gram,
        given_basis,
        given_gram,
        matrix,
        behind,
    )
    return (rotated, norms.reshape(width))


def solution(mesh):
    fine = Mesh(mesh.devices.reshape(2, 4, 8, 4, 2), ("z_hi", "x", "z_lo", "y", "core"))
    return jax.shard_map(
        shards,
        mesh=fine,
        in_specs=(P(ROW, COL), P(COL, None)),
        out_specs=(P(ROW, COL), P(COL)),
        check_vma=False,
    )
```

```python
import functools

import jax
import jax.numpy as jnp
from jax import lax
from jax.experimental import pallas as pl
from jax.experimental.pallas import tpu as pltpu
from jax.sharding import Mesh, PartitionSpec as P

SWEEPS = 4


STEP_GAIN = 3.0
EPSILON = 1e-06

NEAR = ("y", "core")
FAR = "z_lo"
ROW = ("z_lo", "y", "core")
COL = ("z_hi", "x")


DIRECT, RING, TWO, ONE = 272, 224, 264, 264


def send(shard, pairs):
    return lax.ppermute(shard, COL, pairs)


def inside(source, target):
    return [(source, target), (4 + source, 4 + target)]


def across(source, target):
    return [(source, 4 + target), (4 + source, target)]


def product(left, right):
    return jnp.dot(left, right, precision=lax.Precision.HIGH, preferred_element_type=jnp.float32)


def inner_gram(left, right):
    return lax.dot_general(
        left,
        right,
        (((0,), (0,)), ((), ())),
        precision=lax.Precision.HIGH,
        preferred_element_type=jnp.float32,
    )


def spread(piece, axis):
    peers = lax.axis_size(axis)
    copies = jnp.broadcast_to(piece[None], (peers,) + piece.shape)
    return lax.all_to_all(copies, axis, 0, 0, tiled=True)


def near_sum(part):
    near = lax.axis_size(NEAR)
    slices = part.reshape(near, part.shape[0] // near, part.shape[1])
    return jnp.sum(lax.all_to_all(slices, NEAR, 0, 0, tiled=True), axis=0)


def far_sum(piece):
    return jnp.sum(spread(piece, FAR), axis=0)


ALONG = (((1,), (0,)), ((), ()))
DOWN = (((0,), (0,)), ((), ()))


def halves(value):
    high = value.astype(jnp.bfloat16)
    return high, (value - high.astype(jnp.float32)).astype(jnp.bfloat16)


def times(left, right, dims=ALONG):
    def dot(one, other):
        return lax.dot_general(one, other, dims, preferred_element_type=jnp.float32)

    return dot(left[0], right[0]) + (dot(left[0], right[1]) + dot(left[1], right[0]))


def picks(left, chosen, dims=ALONG):
    def dot(one):
        return lax.dot_general(one, chosen, dims, preferred_element_type=jnp.float32)

    return dot(left[0]) + dot(left[1])


def diagonal(value):
    width = value.shape[0]
    down = lax.broadcasted_iota(jnp.int32, (width, width), 0)
    along = lax.broadcasted_iota(jnp.int32, (width, width), 1)
    return jnp.where(down == along, value, 0.0)


def swept(gram, last_gram):
    width = gram.shape[0]
    scale = jnp.sum(jnp.sum(diagonal(gram), axis=0, keepdims=True), axis=1, keepdims=True) / width
    scaled = gram / scale
    down = lax.broadcasted_iota(jnp.int32, (width, width), 0)
    along = lax.broadcasted_iota(jnp.int32, (width, width), 1)
    steps = (along - down).astype(jnp.float32) * (STEP_GAIN / width / width)
    ident = jnp.where(down == along, 1.0, 0.0)
    basis = ident
    for sweep in range(SWEEPS):
        skew = scaled * steps
        pair = halves(skew)
        square = 0.5 * times(pair, pair)
        move = skew + square
        moves = halves(move)
        half_way = scaled + times(halves(scaled), moves)
        basis = ident + move if sweep == 0 else basis + times(halves(basis), moves)
        if sweep < SWEEPS - 1 or last_gram:
            scaled = half_way + times(halves(square - skew), halves(half_way))
    if last_gram:
        return basis, scaled * scale
    return basis, jnp.sum((ident + move) * half_way, axis=0, keepdims=True) * scale


def whole_gram(upper, between, lower):
    return jnp.concatenate(
        [
            jnp.concatenate([upper, between], axis=1),
            jnp.concatenate([between.T, lower], axis=1),
        ],
        axis=0,
    )


def picked(blocks, order, first):
    half = blocks.shape[1]
    gram = whole_gram(blocks[:half], blocks[half : 2 * half], blocks[2 * half :])
    basis, moved = swept(gram, True)
    down = lax.broadcasted_iota(jnp.int32, (2 * half, half), 0)
    chosen = jnp.where(down == order[:, first : first + half], 1.0, 0.0).astype(jnp.bfloat16)
    columns = halves(picks(halves(moved), chosen))
    return picks(halves(basis), chosen), picks(columns, chosen, DOWN)


def turn_kernel(first, blocks_ref, order_ref, basis_ref, gram_ref):
    half = blocks_ref.shape[2]
    basis_ref[...], gram_ref[...] = picked(blocks_ref[...].reshape(3 * half, half), order_ref[...], first)


def turn_pair(blocks, order, first):
    half = blocks.shape[2]
    return pl.pallas_call(
        functools.partial(turn_kernel, first),
        out_shape=(
            jax.ShapeDtypeStruct((2 * half, half), jnp.float32),
            jax.ShapeDtypeStruct((half, half), jnp.float32),
        ),
        compiler_params=pltpu.CompilerParams(vmem_limit_bytes=40 * 2**20),
        cost_estimate=pl.CostEstimate(flops=5 * 10**9, bytes_accessed=4 * 10**5, transcendentals=0),
        name="turn_pair",
    )(blocks, order)


def last_kernel(rows, cross_ref, gram_ref, given_basis_ref, given_gram_ref, kept_ref, given_ref,
                out_ref, norm_ref, high, low):
    half = kept_ref.shape[1]

    @pl.when(pl.program_id(0) == 0)
    def _():
        between = times(halves(cross_ref[...].reshape(2 * half, half)), halves(given_basis_ref[...]), DOWN)
        basis, squares = swept(whole_gram(gram_ref[...], between, given_gram_ref[...]), False)
        norm_ref[...] = jnp.sqrt(jnp.maximum(squares, 0.0) / rows + EPSILON)
        high[...], low[...] = halves(basis)

    pair = jnp.concatenate([kept_ref[...], given_ref[...]], axis=1)
    out_ref[...] = times(halves(pair), (high[...], low[...]))


def sweep_last(rows, cross, gram, given_basis, given_gram, kept, given):
    half = kept.shape[1]
    width = 2 * half
    tile = 256
    full = lambda value: pl.BlockSpec(value.shape, lambda step: (0,) * value.ndim)
    tiles = lambda size: pl.BlockSpec((tile, size), lambda step: (step, 0))
    small = (cross, gram, given_basis, given_gram)
    return pl.pallas_call(
        functools.partial(last_kernel, rows),
        grid=(kept.shape[0] // tile,),
        in_specs=[full(value) for value in small] + [tiles(half), tiles(half)],
        out_specs=(tiles(width), pl.BlockSpec((1, width), lambda step: (0, 0))),
        out_shape=(
            jax.ShapeDtypeStruct((kept.shape[0], width), jnp.float32),
            jax.ShapeDtypeStruct((1, width), jnp.float32),
        ),
        scratch_shapes=[pltpu.VMEM((width, width), jnp.bfloat16)] * 2,
        compiler_params=pltpu.CompilerParams(vmem_limit_bytes=40 * 2**20),
        name="sweep_last",
    )(*small, kept, given)


def first_blocks(matrix):
    half = matrix.shape[1] // 2
    gram = inner_gram(matrix, matrix)
    return jnp.concatenate([gram[:half, :half], gram[:half, half:], gram[half:, half:]], axis=0)


def shards(matrix, keep):
    rows, width = matrix.shape
    half = width // 2
    place = lax.axis_index("x")
    direct, _, two, one = jnp.split(matrix, [DIRECT, DIRECT + RING, DIRECT + RING + TWO])
    turned = send(matrix[DIRECT:], sum([inside(i, (i + 1) % 4) for i in range(4)], []))
    part, two, one = lax.optimization_barrier((first_blocks(matrix), two, one))
    at_two = send(two, inside(3, 2))
    at_one = send(one, inside(3, 1))
    slices = near_sum(part)
    at_two, at_one, slices = lax.optimization_barrier((at_two, at_one, slices))
    crossed_ring = send(turned[:RING], across(0, 0))
    crossed_two = send(at_two, across(2, 0))
    crossed_one = send(at_one, across(1, 0))
    direct = send(direct, [(i, (i + 1) % 8) for i in range(8)])
    slices = far_sum(slices)
    share = slices.shape[0]
    order = jnp.broadcast_to(keep.astype(jnp.float32).reshape(2, half)[None], (4, 2, half)).reshape(8, half)
    arrived = send(jnp.concatenate([slices, order], axis=0), [(i, (i + 1) % 8) for i in range(8)])

    def turn_first(slices, keep):
        return turn_pair(spread(slices, NEAR), keep, 0)

    kept_basis, kept_gram = lax.cond(
        keep[0, 0] >= 0,
        turn_first,
        lambda *_: (jnp.zeros((width, half), jnp.float32), jnp.zeros((half, half), jnp.float32)),
        slices,
        keep,
    )

    direct, crossed_ring, crossed_two, crossed_one, arrived, kept_basis = lax.optimization_barrier(
        (direct, crossed_ring, crossed_two, crossed_one, arrived, kept_basis)
    )
    crossed = jnp.concatenate([crossed_ring, crossed_two, crossed_one], axis=0)
    behind = jnp.concatenate([direct, jnp.where(place == 0, crossed, turned)], axis=0)
    near = lax.axis_size(NEAR)
    cut = width // near
    kept = product(matrix, kept_basis)
    cross = inner_gram(behind, kept).reshape(near, cut, half)
    parts = [cross, jnp.broadcast_to(arrived[None, :share], (near, share, half))]
    parts = lax.all_to_all(jnp.concatenate(parts, axis=1), NEAR, 0, 0, tiled=True)
    cross = far_sum(jnp.sum(parts[:, :cut], axis=0))
    behind_keep = arrived[share : share + 2].reshape(1, width).astype(jnp.int32)
    given_basis, given_gram = turn_pair(parts[:, cut:], behind_keep, half)
    cross, given_basis, given_gram = lax.optimization_barrier((cross, given_basis, given_gram))
    rotated, norms = sweep_last(
        rows * lax.axis_size(ROW),
        spread(cross, NEAR),
        kept_gram,
        given_basis,
        given_gram,
        kept,
        product(behind, given_basis),
    )
    return (rotated, norms.reshape(width))


def solution(mesh):
    fine = Mesh(mesh.devices.reshape(2, 4, 8, 4, 2), ("z_hi", "x", "z_lo", "y", "core"))
    return jax.shard_map(
        shards,
        mesh=fine,
        in_specs=(P(ROW, COL), P(COL, None)),
        out_specs=(P(ROW, COL), P(COL)),
        check_vma=False,
    )
```

```python
import functools

import jax
import jax.numpy as jnp
from jax import lax
from jax.experimental import pallas as pl
from jax.experimental.pallas import tpu as pltpu
from jax.sharding import Mesh, PartitionSpec as P

SWEEPS = 4


STEP_GAIN = 3.0
EPSILON = 1e-06

NEAR = ("y", "core")
FAR = "z_lo"
ROW = ("z_lo", "y", "core")
COL = ("z_hi", "x")


DIRECT, RING, TWO, ONE = 272, 224, 264, 264


def send(shard, pairs):
    return lax.ppermute(shard, COL, pairs)


def inside(source, target):
    return [(source, target), (4 + source, 4 + target)]


def across(source, target):
    return [(source, 4 + target), (4 + source, target)]


def product(left, right):
    return jnp.dot(left, right, precision=lax.Precision.HIGH, preferred_element_type=jnp.float32)


def inner_gram(left, right):
    return lax.dot_general(
        left,
        right,
        (((0,), (0,)), ((), ())),
        precision=lax.Precision.HIGH,
        preferred_element_type=jnp.float32,
    )


def spread(piece, axis):
    peers = lax.axis_size(axis)
    copies = jnp.broadcast_to(piece[None], (peers,) + piece.shape)
    return lax.all_to_all(copies, axis, 0, 0, tiled=True)


def near_sum(part):
    near = lax.axis_size(NEAR)
    slices = part.reshape(near, part.shape[0] // near, part.shape[1])
    return jnp.sum(lax.all_to_all(slices, NEAR, 0, 0, tiled=True), axis=0)


def far_sum(piece):
    return jnp.sum(spread(piece, FAR), axis=0)


ALONG = (((1,), (0,)), ((), ()))
DOWN = (((0,), (0,)), ((), ()))


def halves(value):
    high = value.astype(jnp.bfloat16)
    return high, (value - high.astype(jnp.float32)).astype(jnp.bfloat16)


def times(left, right, dims=ALONG):
    def dot(one, other):
        return lax.dot_general(one, other, dims, preferred_element_type=jnp.float32)

    return dot(left[0], right[0]) + (dot(left[0], right[1]) + dot(left[1], right[0]))


def picks(left, chosen, dims=ALONG):
    def dot(one):
        return lax.dot_general(one, chosen, dims, preferred_element_type=jnp.float32)

    return dot(left[0]) + dot(left[1])


def diagonal(value):
    width = value.shape[0]
    down = lax.broadcasted_iota(jnp.int32, (width, width), 0)
    along = lax.broadcasted_iota(jnp.int32, (width, width), 1)
    return jnp.where(down == along, value, 0.0)


def swept(gram, last_gram):
    width = gram.shape[0]
    scale = jnp.sum(jnp.sum(diagonal(gram), axis=0, keepdims=True), axis=1, keepdims=True) / width
    scaled = gram / scale
    down = lax.broadcasted_iota(jnp.int32, (width, width), 0)
    along = lax.broadcasted_iota(jnp.int32, (width, width), 1)
    steps = (along - down).astype(jnp.float32) * (STEP_GAIN / width / width)
    ident = jnp.where(down == along, 1.0, 0.0)
    basis = ident
    for sweep in range(SWEEPS):
        skew = scaled * steps
        pair = halves(skew)
        square = 0.5 * times(pair, pair)
        move = skew + square
        moves = halves(move)
        half_way = scaled + times(halves(scaled), moves)
        basis = ident + move if sweep == 0 else basis + times(halves(basis), moves)
        if sweep < SWEEPS - 1 or last_gram:
            scaled = half_way + times(halves(square - skew), halves(half_way))
    if last_gram:
        return basis, scaled * scale
    return basis, jnp.sum((ident + move) * half_way, axis=0, keepdims=True) * scale


def whole_gram(upper, between, lower):
    return jnp.concatenate(
        [
            jnp.concatenate([upper, between], axis=1),
            jnp.concatenate([between.T, lower], axis=1),
        ],
        axis=0,
    )


def pair_gram(blocks_ref):
    half = blocks_ref.shape[2]
    blocks = blocks_ref[...].reshape(3 * half, half)
    return whole_gram(blocks[:half], blocks[half : 2 * half], blocks[2 * half :])


def turn_kernel(first, blocks_ref, order_ref, basis_ref):
    half = blocks_ref.shape[2]
    basis, _ = swept(pair_gram(blocks_ref), False)
    down = lax.broadcasted_iota(jnp.int32, (2 * half, half), 0)
    chosen = jnp.where(down == order_ref[:, first : first + half], 1.0, 0.0).astype(jnp.bfloat16)
    basis_ref[...] = picks(halves(basis), chosen)


def turn_pair(blocks, order, first):
    half = blocks.shape[2]
    return pl.pallas_call(
        functools.partial(turn_kernel, first),
        out_shape=jax.ShapeDtypeStruct((2 * half, half), jnp.float32),
        compiler_params=pltpu.CompilerParams(vmem_limit_bytes=40 * 2**20),
        cost_estimate=pl.CostEstimate(flops=5 * 10**9, bytes_accessed=4 * 10**5, transcendentals=0),
        name="turn_pair",
    )(blocks, order)


def gram_kernel(own_ref, kept_ref, behind_ref, given_ref, own_out_ref, behind_out_ref):
    for blocks_ref, basis_ref, out_ref in ((own_ref, kept_ref, own_out_ref), (behind_ref, given_ref, behind_out_ref)):
        basis = halves(basis_ref[...])
        out_ref[...] = times(basis, halves(times(halves(pair_gram(blocks_ref)), basis)), DOWN)


def turned_grams(own, kept, behind, given):
    half = kept.shape[1]
    return pl.pallas_call(
        gram_kernel,
        out_shape=(jax.ShapeDtypeStruct((half, half), jnp.float32),) * 2,
        compiler_params=pltpu.CompilerParams(vmem_limit_bytes=40 * 2**20),
        cost_estimate=pl.CostEstimate(flops=10**9, bytes_accessed=8 * 10**5, transcendentals=0),
        name="turned_grams",
    )(own, kept, behind, given)


def last_kernel(rows, cross_ref, gram_ref, given_basis_ref, given_gram_ref, kept_ref, given_ref,
                out_ref, norm_ref, high, low):
    half = kept_ref.shape[1]

    @pl.when(pl.program_id(0) == 0)
    def _():
        between = times(halves(cross_ref[...].reshape(2 * half, half)), halves(given_basis_ref[...]), DOWN)
        basis, squares = swept(whole_gram(gram_ref[...], between, given_gram_ref[...]), False)
        norm_ref[...] = jnp.sqrt(jnp.maximum(squares, 0.0) / rows + EPSILON)
        high[...], low[...] = halves(basis)

    pair = jnp.concatenate([kept_ref[...], given_ref[...]], axis=1)
    out_ref[...] = times(halves(pair), (high[...], low[...]))


def sweep_last(rows, cross, gram, given_basis, given_gram, kept, given):
    half = kept.shape[1]
    width = 2 * half
    tile = 256
    full = lambda value: pl.BlockSpec(value.shape, lambda step: (0,) * value.ndim)
    tiles = lambda size: pl.BlockSpec((tile, size), lambda step: (step, 0))
    small = (cross, gram, given_basis, given_gram)
    return pl.pallas_call(
        functools.partial(last_kernel, rows),
        grid=(kept.shape[0] // tile,),
        in_specs=[full(value) for value in small] + [tiles(half), tiles(half)],
        out_specs=(tiles(width), pl.BlockSpec((1, width), lambda step: (0, 0))),
        out_shape=(
            jax.ShapeDtypeStruct((kept.shape[0], width), jnp.float32),
            jax.ShapeDtypeStruct((1, width), jnp.float32),
        ),
        scratch_shapes=[pltpu.VMEM((width, width), jnp.bfloat16)] * 2,
        compiler_params=pltpu.CompilerParams(vmem_limit_bytes=40 * 2**20),
        name="sweep_last",
    )(*small, kept, given)


def first_blocks(matrix):
    half = matrix.shape[1] // 2
    gram = inner_gram(matrix, matrix)
    return jnp.concatenate([gram[:half, :half], gram[:half, half:], gram[half:, half:]], axis=0)


def shards(matrix, keep):
    rows, width = matrix.shape
    half = width // 2
    place = lax.axis_index("x")
    direct, _, two, one = jnp.split(matrix, [DIRECT, DIRECT + RING, DIRECT + RING + TWO])
    turned = send(matrix[DIRECT:], sum([inside(i, (i + 1) % 4) for i in range(4)], []))
    part, two, one = lax.optimization_barrier((first_blocks(matrix), two, one))
    at_two = send(two, inside(3, 2))
    at_one = send(one, inside(3, 1))
    slices = near_sum(part)
    at_two, at_one, slices = lax.optimization_barrier((at_two, at_one, slices))
    crossed_ring = send(turned[:RING], across(0, 0))
    crossed_two = send(at_two, across(2, 0))
    crossed_one = send(at_one, across(1, 0))
    direct = send(direct, [(i, (i + 1) % 8) for i in range(8)])
    slices = far_sum(slices)
    share = slices.shape[0]
    order = jnp.broadcast_to(keep.astype(jnp.float32).reshape(2, half)[None], (4, 2, half)).reshape(8, half)
    arrived = send(jnp.concatenate([slices, order], axis=0), [(i, (i + 1) % 8) for i in range(8)])

    def turn_first(slices, keep):
        blocks = spread(slices, NEAR)
        return turn_pair(blocks, keep, 0), blocks

    kept_basis, own_blocks = lax.cond(
        keep[0, 0] >= 0,
        turn_first,
        lambda *_: (jnp.zeros((width, half), jnp.float32), jnp.zeros((8, share, half), jnp.float32)),
        slices,
        keep,
    )

    direct, crossed_ring, crossed_two, crossed_one, arrived, kept_basis = lax.optimization_barrier(
        (direct, crossed_ring, crossed_two, crossed_one, arrived, kept_basis)
    )
    crossed = jnp.concatenate([crossed_ring, crossed_two, crossed_one], axis=0)
    behind = jnp.concatenate([direct, jnp.where(place == 0, crossed, turned)], axis=0)
    near = lax.axis_size(NEAR)
    cut = width // near
    kept = product(matrix, kept_basis)
    cross = inner_gram(behind, kept).reshape(near, cut, half)
    parts = [cross, jnp.broadcast_to(arrived[None, :share], (near, share, half))]
    parts = lax.all_to_all(jnp.concatenate(parts, axis=1), NEAR, 0, 0, tiled=True)
    cross = far_sum(jnp.sum(parts[:, :cut], axis=0))
    behind_keep = arrived[share : share + 2].reshape(1, width).astype(jnp.int32)
    behind_blocks = parts[:, cut:]
    given_basis = turn_pair(behind_blocks, behind_keep, half)
    kept_gram, given_gram = turned_grams(own_blocks, kept_basis, behind_blocks, given_basis)
    cross, given_basis, kept_gram, given_gram = lax.optimization_barrier(
        (cross, given_basis, kept_gram, given_gram)
    )
    rotated, norms = sweep_last(
        rows * lax.axis_size(ROW),
        spread(cross, NEAR),
        kept_gram,
        given_basis,
        given_gram,
        kept,
        product(behind, given_basis),
    )
    return (rotated, norms.reshape(width))


def solution(mesh):
    fine = Mesh(mesh.devices.reshape(2, 4, 8, 4, 2), ("z_hi", "x", "z_lo", "y", "core"))
    return jax.shard_map(
        shards,
        mesh=fine,
        in_specs=(P(ROW, COL), P(COL, None)),
        out_specs=(P(ROW, COL), P(COL)),
        check_vma=False,
    )
```
